256 devices in a mesh: dp: 4 (over z_hi, core), seq: 64 (over y, x, z_lo).
Axes of the slice: x: 4, y: 4, z: 8 (z_hi: 2, z_lo: 4; z = z_hi * 4 + z_lo), core: 2. Of those that a mesh axis runs over, the one named last changes fastest.
Arguments:
- tokens: bfloat16 [4, 16384, 1024], P('dp', 'seq'), may hold values from -6 to 6
- cotangent: bfloat16 [4, 16384, 1024], P('dp', 'seq'), may hold values from -6 to 6
- first_factor: bfloat16 [64, 256, 256], P('seq'), may hold values from -0.375 to 0.375
- second_factor: bfloat16 [64, 256, 64], P(None, 'seq'), may hold values from -0.75 to 0.75
- norm_gain: float32 [1024], replicated, may hold values from 0.25 to 1.75
- gate_scale: float32 [1024], replicated, may hold values from -4 to 4
- gate_bias: float32 [1024], replicated, may hold values from -4 to 4
- mlp_gain: float32 [1024], replicated, may hold values from 0.25 to 1.75
- gate_weight: bfloat16 [8, 128, 512], replicated, may hold values from -0.5 to 0.5
- up_weight: bfloat16 [8, 128, 512], replicated, may hold values from -0.5 to 0.5
- down_weight: bfloat16 [8, 128, 512], replicated, may hold values from -0.25 to 0.25
Outputs:
- grad_tokens: bfloat16 [4, 16384, 1024], P('dp', 'seq')
- grad_first: float32 [64, 256, 256], P('seq', None, 'dp')
- grad_second: float32 [64, 256, 64], P(None, 'seq', 'dp')
- grad_gate: float32 [8, 128, 512], P('dp', None, 'seq')
- grad_up: float32 [8, 128, 512], P('dp', None, 'seq')
- grad_down: float32 [8, 128, 512], P('dp', None, 'seq')
The draws below stay inside these ranges and needn't reach their ends.
All inputs are finite; a program needn't handle non-finite values.
Results may differ from the reference program's by a relative error of at most 0.017.
Values may be sent and summed in bfloat16 or wider, within the bound.
No kernel may reach another device: no remote copies, remote signals or barrier semaphores. Data moves between devices by JAX's collectives and lax.ppermute only.
A program may use at most 128 MiB of HBM per device.

```python
import jax
import jax.numpy as jnp
from jax import lax

D = 1024
MB = 8
BLK = 256
SEQS = 4
L = 16384
NB = 64
DB = 128
HB = 512


def block_levels(rng, extent, shards, least, largest):
    loudness = 1.0
    for dim, shards_of in shards:
        steps = jax.random.uniform(jax.random.fold_in(jax.random.fold_in(rng, 6), dim), (shards_of,), jnp.float32, least / len(shards), largest / len(shards))
        loudness = loudness * jnp.repeat(jnp.exp(steps), extent[dim] // shards_of).reshape((-1,) + (1,) * (len(extent) - 1 - dim))
    return loudness


def noise(rng, extent, deviation, bound, cuts=(), dtype=jnp.bfloat16):
    drawn = deviation * jax.random.normal(rng, extent, jnp.float32)
    if cuts:
        drawn = drawn * block_levels(rng, extent, cuts, -0.22, 0.18)
    return jnp.clip(drawn, -bound, bound).astype(dtype)


def setup_inputs(seed: int = 0) -> dict:
    seeds = jax.random.split(jax.random.key(seed), 12)
    return {
        "tokens": noise(seeds[0], (SEQS, L, D), 1.0, 6.0, ((0, 4), (1, 64))),
        "cotangent": noise(seeds[1], (SEQS, L, D), 1.0, 6.0, ((0, 4), (1, 64))),
        "first_factor": noise(seeds[2], (NB, BLK, BLK), BLK ** -0.5, 0.375, ((0, 64),)),
        "second_factor": noise(seeds[3], (NB, BLK, NB), NB ** -0.5, 0.75, ((1, 64),)),
        "norm_gain": jnp.clip(1.0 + 0.15 * jax.random.normal(seeds[4], (D,), jnp.float32), 0.25, 1.75),
        "gate_scale": noise(seeds[5], (D,), 1.0, 4.0, (), jnp.float32),
        "gate_bias": noise(seeds[6], (D,), 1.0, 4.0, (), jnp.float32),
        "mlp_gain": jnp.clip(1.0 + 0.15 * jax.random.normal(seeds[7], (D,), jnp.float32), 0.25, 1.75),
        "gate_weight": noise(seeds[8], (MB, DB, HB), DB ** -0.5, 0.5),
        "up_weight": noise(seeds[9], (MB, DB, HB), DB ** -0.5, 0.5),
        "down_weight": noise(seeds[10], (MB, DB, HB), HB ** -0.5, 0.25),
    }


epsilon = 1e-05

def inverse_rms(values):
    return lax.rsqrt(lax.optimization_barrier(jnp.mean(values * values, axis=-1, keepdims=True)) + epsilon)

def norm_backward(grad_normed, normed_values, inverse):
    return inverse * (grad_normed - normed_values * lax.optimization_barrier(jnp.mean(grad_normed * normed_values, axis=-1, keepdims=True)))

def wide_einsum(pattern, left_side, right_side):
    return jnp.einsum(pattern, left_side.astype(jnp.float32), right_side.astype(jnp.float32))

def one_sequence(inputs, upstream, first_factor, second_factor, norm_gain, gate_scale, gate_bias, mlp_gain, gate_weight, up_weight, down_weight):
    inputs_wide = inputs.astype(jnp.float32)
    first_inverse = inverse_rms(inputs_wide)
    first_normed = inputs_wide * first_inverse
    normed_tokens = (first_normed * norm_gain).astype(jnp.bfloat16)
    blocked = normed_tokens.reshape(NB, BLK, D)
    section_one = wide_einsum('bij,bjd->bid', first_factor, blocked).astype(jnp.bfloat16)
    mixed_seq = wide_einsum('cib,bid->cid', second_factor, section_one).astype(jnp.bfloat16).reshape(L, D)
    mixed_wide = mixed_seq.astype(jnp.float32)
    gate_open = jax.nn.sigmoid(normed_tokens.astype(jnp.float32) * gate_scale + gate_bias)
    after_mix = (inputs_wide + mixed_wide * gate_open).astype(jnp.bfloat16)
    after_wide = after_mix.astype(jnp.float32)
    second_inverse = inverse_rms(after_wide)
    second_normed = after_wide * second_inverse
    mlp_input = (second_normed * mlp_gain).astype(jnp.bfloat16).reshape(L, MB, DB)
    pre_gate = wide_einsum('tkd,kdh->tkh', mlp_input, gate_weight)
    pre_up = wide_einsum('tkd,kdh->tkh', mlp_input, up_weight)
    sig_gate = jax.nn.sigmoid(pre_gate)
    hidden = (pre_gate * sig_gate * pre_up).astype(jnp.bfloat16)
    permuted = jnp.transpose(hidden, (0, 2, 1)).reshape(L, MB, HB)
    upstream_wide = upstream.astype(jnp.float32)
    upstream_blocks = upstream.reshape(L, MB, DB)
    grad_perm = wide_einsum('tkd,kdh->tkh', upstream_blocks, down_weight).astype(jnp.bfloat16)
    down_term = wide_einsum('tkd,tkh->kdh', upstream_blocks, permuted)
    grad_hidden = jnp.transpose(grad_perm.reshape(L, HB, MB), (0, 2, 1)).astype(jnp.float32)
    grad_gate_pre = (grad_hidden * pre_up * sig_gate * (1.0 + pre_gate * (1.0 - sig_gate))).astype(jnp.bfloat16)
    grad_up_pre = (grad_hidden * pre_gate * sig_gate).astype(jnp.bfloat16)
    gate_term = wide_einsum('tkd,tkh->kdh', mlp_input, grad_gate_pre)
    up_term = wide_einsum('tkd,tkh->kdh', mlp_input, grad_up_pre)
    grad_inner = wide_einsum('tkh,kdh->tkd', grad_gate_pre, gate_weight) + wide_einsum('tkh,kdh->tkd', grad_up_pre, up_weight)
    grad_inner = grad_inner.reshape(L, D)
    grad_after = (upstream_wide + norm_backward(grad_inner * mlp_gain, second_normed, second_inverse)).astype(jnp.bfloat16)
    grad_after_wide = grad_after.astype(jnp.float32)
    grad_mixed = (grad_after_wide * gate_open).astype(jnp.bfloat16)
    grad_open = grad_after_wide * mixed_wide * gate_open * (1.0 - gate_open)
    grad_mixed_blocks = grad_mixed.reshape(NB, BLK, D)
    grad_section = wide_einsum('cib,cid->bid', second_factor, grad_mixed_blocks).astype(jnp.bfloat16)
    second_term = wide_einsum('cid,bid->cib', grad_mixed_blocks, section_one)
    first_term = wide_einsum('bid,bjd->bij', grad_section, blocked)
    grad_normed = wide_einsum('bij,bid->bjd', first_factor, grad_section).reshape(L, D) + grad_open * gate_scale
    grad_inputs = (grad_after_wide + norm_backward(grad_normed * norm_gain, first_normed, first_inverse)).astype(jnp.bfloat16)
    return (grad_inputs, first_term, second_term, gate_term, up_term, down_term)

def reference(tokens, cotangent, first_factor, second_factor, norm_gain, gate_scale, gate_bias, mlp_gain, gate_weight, up_weight, down_weight):
    grads_list = []
    first_total = jnp.zeros((NB, BLK, BLK), jnp.float32)
    second_total = jnp.zeros((NB, BLK, NB), jnp.float32)
    gate_total = jnp.zeros((MB, DB, HB), jnp.float32)
    up_total = jnp.zeros((MB, DB, HB), jnp.float32)
    down_total = jnp.zeros((MB, DB, HB), jnp.float32)
    for sequence in range(SEQS):
        outcome = one_sequence(tokens[sequence], cotangent[sequence], first_factor, second_factor, norm_gain, gate_scale, gate_bias, mlp_gain, gate_weight, up_weight, down_weight)
        grads_list.append(outcome[0])
        first_total = first_total + outcome[1]
        second_total = second_total + outcome[2]
        gate_total = gate_total + outcome[3]
        up_total = up_total + outcome[4]
        down_total = down_total + outcome[5]
    factor_weight = (SEQS * D) ** (-0.5)
    mlp_weight = (SEQS * L) ** (-0.5)
    return (jnp.stack(grads_list), first_total * factor_weight, second_total * factor_weight, gate_total * mlp_weight, up_total * mlp_weight, down_total * mlp_weight)
```

```python
import functools

import jax
import jax.numpy as jnp
from jax import lax
from jax.experimental import pallas as pl
from jax.experimental.pallas import tpu as pltpu
from jax.sharding import Mesh, PartitionSpec as P

EPS = 1e-05
BF = jnp.bfloat16
F32 = jnp.float32
SEQ = ("y", "x", "zl")
DP = ("zh", "core")

ROWS = 256
WIDTH = 1024
HALF = 512
CHUNKS = 64
MB = 8
HB = 512
DB = 128


def iota(shape, dim):
    return lax.broadcasted_iota(jnp.int32, shape, dim)


def one_hot(condition):
    return jnp.where(condition, 1.0, 0.0).astype(BF)


def nn(a, b):
    return jnp.dot(a, b, preferred_element_type=F32)


def nt(a, b):
    return lax.dot_general(a, b, (((1,), (1,)), ((), ())), preferred_element_type=F32)


def tn(a, b):
    return lax.dot_general(a, b, (((0,), (0,)), ((), ())), preferred_element_type=F32)


def to_chunks(value):
    row = iota((HALF, HALF), 0)
    col = iota((HALF, HALF), 1)
    perm = one_hot(col == (row & 4) * 64 + (row >> 3) * 4 + (row & 3))
    stacked = jnp.concatenate([value[:, :HALF], value[:, HALF:]], axis=0)
    return nn(perm, stacked).astype(BF)


def from_chunks(chunked):
    row = iota((HALF, HALF), 0)
    col = iota((HALF, HALF), 1)
    perm = one_hot(col == ((row >> 2) & 63) * 8 + (row >> 8) * 4 + (row & 3))
    stacked = nn(perm, chunked)
    return jnp.concatenate([stacked[:ROWS], stacked[ROWS:]], axis=1)


def inverse_rms(values):
    return lax.rsqrt(jnp.mean(values * values, axis=-1, keepdims=True) + EPS)


def norm_section(tok_ref, first_ref, gain_ref, normed_ref, sec_ref):
    wide = tok_ref[...].astype(F32)
    normed = (wide * inverse_rms(wide) * gain_ref[...]).astype(BF)
    normed_ref[...] = normed
    sec_ref[...] = to_chunks(nn(first_ref[...], normed).astype(BF))


def spread_rows():
    row = iota((HALF, ROWS), 0)
    col = iota((HALF, ROWS), 1)
    return one_hot(col == (row >> 3) * 4 + (row & 3))


def block_mask():
    return (iota((HALF, HALF), 0) & 7) == (iota((HALF, HALF), 1) & 7)


def prepare(gate_ref, up_ref, down_ref, second_ref, wt_ref, dt_ref, m_ref, mt_ref):
    row = iota((HB, HB), 0)
    col = iota((HB, HB), 1)
    same = one_hot(row == col)
    regroup = one_hot(col == (row & 63) * 8 + (row >> 6))
    for k in range(MB):
        wt_ref[k, 0:HB, :] = nt(same, gate_ref[k]).astype(BF)
        wt_ref[k, HB:, :] = nt(same, up_ref[k]).astype(BF)
        dt_ref[k] = nt(regroup, down_ref[k]).astype(BF)
    rows = spread_rows()
    lanes = one_hot((iota((HALF, CHUNKS), 0) >> 3) == iota((HALF, CHUNKS), 1))
    mask = block_mask()
    second = second_ref[...]
    tall = nn(rows, second).astype(BF)
    m_ref[...] = jnp.where(mask, nt(tall, lanes), 0.0).astype(BF)
    tall_back = nt(lanes, second).astype(BF)
    mt_ref[...] = jnp.where(mask, nt(tall_back, rows), 0.0).astype(BF)


def mix(m_ref, x_ref, out_ref):
    out_ref[...] = nn(m_ref[...], x_ref[...]).astype(BF)


def second_grad(sec_ref, gmix_ref, out_ref):
    pairs = nt(sec_ref[...], gmix_ref[...])
    pairs = jnp.where(block_mask(), pairs, 0.0).astype(BF)
    gather = one_hot(iota((CHUNKS, HALF), 0) == (iota((CHUNKS, HALF), 1) >> 3))
    picked = nn(gather, pairs).astype(BF)
    out_ref[...] = nn(picked, spread_rows()).astype(BF)


def mlp(
    mixx_ref, tok_ref, cot_ref, normed_ref, scale_ref, bias_ref, gain_ref,
    wt_ref, dt_ref, gate_ref, up_ref,
    gx_ref, gres_ref, gopen_ref, grads_ref,
    gs, hs, inner_s, gin_s,
):
    mixed = from_chunks(mixx_ref[...])
    opened = jax.nn.sigmoid(normed_ref[...].astype(F32) * scale_ref[...] + bias_ref[...])
    resid = (tok_ref[...].astype(F32) + mixed * opened).astype(BF).astype(F32)
    inverse = inverse_rms(resid)
    inner_s[...] = (resid * inverse * gain_ref[...]).astype(BF)
    for kb in range(MB):
        g_perm = nt(dt_ref[kb], cot_ref[:, kb * DB : (kb + 1) * DB]).astype(BF)
        for k in range(MB):
            gs[k, kb * 64 : (kb + 1) * 64, :] = g_perm[k * 64 : (k + 1) * 64]
    for k in range(MB):
        inner = inner_s[:, k * DB : (k + 1) * DB]
        pre = nt(wt_ref[k], inner)
        pre_gate = pre[:HB]
        pre_up = pre[HB:]
        sig = jax.nn.sigmoid(pre_gate)
        silu = pre_gate * sig
        g_hidden = gs[k].astype(F32)
        hidden = (silu * pre_up).astype(BF)
        for kb in range(MB):
            hs[kb, k * 64 : (k + 1) * 64, :] = hidden[kb * 64 : (kb + 1) * 64]
        g_gate = (g_hidden * pre_up * (sig * (1.0 + pre_gate * (1.0 - sig)))).astype(BF)
        g_up = (g_hidden * silu).astype(BF)
        zh, core, part = k >> 2, (k >> 1) & 1, k & 1
        grads_ref[core, 0, zh, part] = nn(g_gate, inner).astype(BF)
        grads_ref[core, 1, zh, part] = nn(g_up, inner).astype(BF)
        g_inner = nn(gate_ref[k], g_gate) + nn(up_ref[k], g_up)
        gin_s[:, k * DB : (k + 1) * DB] = g_inner.T
    row = iota((HB, HB), 0)
    col = iota((HB, HB), 1)
    restore = one_hot(col == (row & 7) * 64 + (row >> 3))
    for kb in range(MB):
        zh, core, part = kb >> 2, (kb >> 1) & 1, kb & 1
        term = nn(hs[kb], cot_ref[:, kb * DB : (kb + 1) * DB]).astype(BF)
        grads_ref[core, 2, zh, part] = nn(restore, term).astype(BF)
    d_norm = gin_s[...] * gain_ref[...]
    norm2 = resid * inverse
    back = inverse * (d_norm - norm2 * jnp.mean(d_norm * norm2, axis=-1, keepdims=True))
    g_resid = (cot_ref[...].astype(F32) + back).astype(BF)
    gres_ref[...] = g_resid
    wide = g_resid.astype(F32)
    gx_ref[...] = to_chunks((wide * opened).astype(BF))
    gopen_ref[...] = wide * mixed * opened * (1.0 - opened) * scale_ref[...]


def first_grad(gsx_ref, normed_ref, gsec_ref, out_ref):
    gsec = from_chunks(gsx_ref[...]).astype(BF)
    gsec_ref[...] = gsec
    out_ref[...] = nt(normed_ref[...], gsec).astype(BF)


def finish(gsec_ref, first_ref, tok_ref, gres_ref, gopen_ref, gain_ref, out_ref):
    d_norm = (tn(first_ref[...], gsec_ref[...]) + gopen_ref[...]) * gain_ref[...]
    wide = tok_ref[...].astype(F32)
    inverse = inverse_rms(wide)
    normed = wide * inverse
    back = inverse * (d_norm - normed * jnp.mean(d_norm * normed, axis=-1, keepdims=True))
    out_ref[...] = (gres_ref[...].astype(F32) + back).astype(BF)


def call(kernel, outs, flops, scratch=(), vmem=24):
    def run(*args):
        moved = sum(a.size * a.dtype.itemsize for a in args)
        moved += sum(o.size * o.dtype.itemsize for o in outs)
        return pl.pallas_call(
            kernel,
            out_shape=outs if len(outs) > 1 else outs[0],
            scratch_shapes=scratch,
            compiler_params=pltpu.CompilerParams(vmem_limit_bytes=vmem * 2**20),
            cost_estimate=pl.CostEstimate(flops=flops, bytes_accessed=moved, transcendentals=0),
            name=kernel.__name__,
        )(*args)

    return run


def struct(shape, dtype=BF):
    return jax.ShapeDtypeStruct(shape, dtype)


def exchange(chunked, axis_names, count):
    return lax.all_to_all(chunked, axis_names, 0, 0, tiled=True)


def seq_exchange(value):
    return exchange(value.reshape(CHUNKS, 8, HALF), SEQ, CHUNKS).reshape(HALF, HALF)


def dp_sum(terms):
    me = lax.axis_index(DP)
    total = lax.dynamic_index_in_dim(terms, me, 0, keepdims=False).astype(F32)
    for step in (1, 2, 3):
        piece = lax.dynamic_index_in_dim(terms, me ^ step, 0, keepdims=False)
        got = lax.ppermute(piece, DP, [(i, i ^ step) for i in range(4)])
        total = total + got.astype(F32)
    return total


def body(
    tokens, cotangent, first_factor, second_factor, norm_gain, gate_scale, gate_bias,
    mlp_gain, gate_weight, up_weight, down_weight,
):
    tok = tokens.reshape(ROWS, WIDTH)
    cot = cotangent.reshape(ROWS, WIDTH)
    first = first_factor.reshape(ROWS, ROWS)
    second = second_factor.reshape(ROWS, CHUNKS)
    gain1 = norm_gain.reshape(1, WIDTH)
    scale = gate_scale.reshape(1, WIDTH)
    bias = gate_bias.reshape(1, WIDTH)
    gain2 = mlp_gain.reshape(1, WIDTH)
    square = struct((HALF, HALF))

    normed, sec = call(norm_section, (struct((ROWS, WIDTH)), square), 10**9)(tok, first, gain1)
    wt, dt, m, mt = call(
        prepare,
        (struct((MB, 2 * HB, DB)), struct((MB, HB, DB)), square, square),
        2 * 10**9,
    )(gate_weight, up_weight, down_weight, second)
    sec_cols = seq_exchange(sec)
    mixed_cols = call(mix, (square,), 3 * 10**8)(m, sec_cols)
    mixx = seq_exchange(mixed_cols)
    gmix, g_resid, g_open, grads = call(
        mlp,
        (
            square,
            struct((ROWS, WIDTH)),
            struct((ROWS, WIDTH), F32),
            struct((2, 3, 2, 2, HB, DB)),
        ),
        8 * 10**9,
        scratch=[
            pltpu.VMEM((MB, HB, ROWS), BF),
            pltpu.VMEM((MB, HB, ROWS), BF),
            pltpu.VMEM((ROWS, WIDTH), BF),
            pltpu.VMEM((ROWS, WIDTH), F32),
        ],
        vmem=44,
    )(mixx, tok, cot, normed, scale, bias, gain2, wt, dt, gate_weight, up_weight)

    gmix_cols = seq_exchange(gmix)
    gsec_cols = call(mix, (square,), 3 * 10**8)(mt, gmix_cols)
    gsx = seq_exchange(gsec_cols)
    second_t = call(second_grad, (struct((CHUNKS, ROWS)),), 5 * 10**8)(sec_cols, gmix_cols)
    gsec, first_t = call(first_grad, (struct((ROWS, WIDTH)), struct((ROWS, ROWS))), 5 * 10**8)(
        gsx, normed
    )
    grad_inputs = call(finish, (struct((ROWS, WIDTH)),), 2 * 10**8)(
        gsec, first, tok, g_resid, g_open, gain1
    )

    core = lax.axis_index("core")
    kept = lax.dynamic_index_in_dim(grads, core, 0, keepdims=False)
    given = lax.dynamic_index_in_dim(grads, 1 - core, 0, keepdims=False)
    got = lax.ppermute(given, "core", [(0, 1), (1, 0)])
    pair = (kept.astype(F32) + got.astype(F32)).astype(BF)
    pair = pair.reshape(3, 2, 2, 16, 32, DB).transpose(3, 0, 1, 2, 4, 5).reshape(16, 384, DB)
    plane = exchange(pair, ("y", "x"), 16).astype(F32).sum(0).astype(BF)
    plane = plane.reshape(3, 2, 2, 4, 8, DB).transpose(1, 3, 0, 2, 4, 5).reshape(8, 48, DB)
    whole = exchange(plane, ("zh", "zl"), 8).astype(F32).sum(0)
    mlp_weight = (4 * ROWS * CHUNKS) ** (-0.5)
    whole = (whole * mlp_weight).reshape(3, 2, 8, DB).transpose(0, 1, 3, 2)

    factor_weight = (4 * WIDTH) ** (-0.5)
    grad_second = dp_sum(second_t.reshape(4, 16, ROWS)) * factor_weight
    grad_first = dp_sum(first_t.reshape(4, 64, ROWS)) * factor_weight
    return (
        grad_inputs[None],
        grad_first.T[None],
        grad_second.T.reshape(CHUNKS, 4, 16),
        whole[0],
        whole[1],
        whole[2],
    )


def solution(mesh):
    fine = Mesh(mesh.devices.reshape(2, 2, 4, 4, 4), ("zh", "core", "y", "x", "zl"))
    placed = (
        P(DP, SEQ, None),
        P(DP, SEQ, None),
        P(SEQ, None, None),
        P(None, SEQ, None),
    ) + (P(),) * 7
    return jax.shard_map(
        body,
        mesh=fine,
        in_specs=placed,
        out_specs=(
            P(DP, SEQ, None),
            P(SEQ, None, DP),
            P(None, SEQ, DP),
            P(DP, None, SEQ),
            P(DP, None, SEQ),
            P(DP, None, SEQ),
        ),
        check_vma=False,
    )
```

```python
import functools

import jax
import jax.numpy as jnp
from jax import lax
from jax.experimental import pallas as pl
from jax.experimental.pallas import tpu as pltpu
from jax.sharding import Mesh, PartitionSpec as P

EPS = 1e-05
SUM_X_COST = 2 * 10**10
BF = jnp.bfloat16
F32 = jnp.float32
SEQ = ("y", "x", "zl")
DP = ("zh", "core")

ROWS = 256
WIDTH = 1024
HALF = 512
CHUNKS = 64
MB = 8
HB = 512
DB = 128


def iota(shape, dim):
    return lax.broadcasted_iota(jnp.int32, shape, dim)


def one_hot(condition):
    return jnp.where(condition, 1.0, 0.0).astype(BF)


def nn(a, b):
    return jnp.dot(a, b, preferred_element_type=F32)


def nt(a, b):
    return lax.dot_general(a, b, (((1,), (1,)), ((), ())), preferred_element_type=F32)


def tn(a, b):
    return lax.dot_general(a, b, (((0,), (0,)), ((), ())), preferred_element_type=F32)


def to_chunks(value):
    row = iota((ROWS, ROWS), 0)
    col = iota((ROWS, ROWS), 1)
    perm = one_hot(col == (row & 4) * 32 + (row >> 3) * 4 + (row & 3))
    blocks = []
    for start in range(0, value.shape[0], 128):
        rows = value[start : start + 128]
        stacked = jnp.concatenate([rows[:, :HALF], rows[:, HALF:]], axis=0)
        blocks.append(nn(perm, stacked).astype(BF))
    return jnp.concatenate(blocks, axis=0)


def from_chunks(chunked):
    row = iota((ROWS, ROWS), 0)
    col = iota((ROWS, ROWS), 1)
    perm = one_hot(col == ((row >> 2) & 31) * 8 + (row >> 7) * 4 + (row & 3))
    blocks = []
    for start in range(0, chunked.shape[0], 256):
        stacked = nn(perm, chunked[start : start + 256])
        blocks.append(jnp.concatenate([stacked[:128], stacked[128:]], axis=1))
    return jnp.concatenate(blocks, axis=0)


def sigmoid(value):
    return 0.5 * jnp.tanh(0.5 * value) + 0.5


def inverse_rms(values):
    return lax.rsqrt(jnp.mean(values * values, axis=-1, keepdims=True) + EPS)


def norm_section(tok_ref, first_ref, gain_ref, normed_ref, sec_ref):
    wide = tok_ref[...].astype(F32)
    normed = (wide * inverse_rms(wide) * gain_ref[...]).astype(BF)
    normed_ref[...] = normed
    sec_ref[...] = to_chunks(nn(first_ref[...], normed).astype(BF))


def spread_rows():
    row = iota((HALF, ROWS), 0)
    col = iota((HALF, ROWS), 1)
    return one_hot(col == (row >> 3) * 4 + (row & 3))


def block_mask():
    return (iota((HALF, HALF), 0) & 7) == (iota((HALF, HALF), 1) & 7)


def block_of():
    return one_hot((iota((HALF, CHUNKS), 0) >> 3) == iota((HALF, CHUNKS), 1))


def prepare_mix(second_ref, m_ref):
    tall = nn(spread_rows(), second_ref[...]).astype(BF)
    m_ref[...] = jnp.where(block_mask(), nt(tall, block_of()), 0.0).astype(BF)


def mix_back(second_ref, x_ref, out_ref):
    tall = nt(block_of(), second_ref[...]).astype(BF)
    back = jnp.where(block_mask(), nt(tall, spread_rows()), 0.0).astype(BF)
    out_ref[...] = nn(back, x_ref[...]).astype(BF)


def prepare_mlp(gate_ref, up_ref, down_ref, cot_ref, wt_ref, gs_ref):
    row = iota((HB, HB), 0)
    col = iota((HB, HB), 1)
    same = one_hot(row == col)
    regroup = one_hot(col == (row & 63) * 8 + (row >> 6))
    for k in range(MB):
        wt_ref[k, 0:HB, :] = nt(same, gate_ref[k]).astype(BF)
        wt_ref[k, HB:, :] = nt(same, up_ref[k]).astype(BF)
    for kb in range(MB):
        down = nt(regroup, down_ref[kb]).astype(BF)
        g_perm = nt(down, cot_ref[:, kb * DB : (kb + 1) * DB]).astype(BF)
        for k in range(MB):
            gs_ref[k, kb * 64 : (kb + 1) * 64, :] = g_perm[k * 64 : (k + 1) * 64]


def mix(m_ref, x_ref, out_ref):
    out_ref[...] = nn(m_ref[...], x_ref[...]).astype(BF)


def second_grad(sec_ref, gmix_ref, out_ref):
    pairs = nt(sec_ref[...], gmix_ref[...])
    pairs = jnp.where(block_mask(), pairs, 0.0).astype(BF)
    gather = one_hot(iota((CHUNKS, HALF), 0) == (iota((CHUNKS, HALF), 1) >> 3))
    picked = nn(gather, pairs).astype(BF)
    out_ref[...] = nn(picked, spread_rows()).astype(BF)


def mlp(
    place_ref, scale_ref, bias_ref, gain_ref, mixx_ref,
    tok_hbm, normed_hbm, wt_hbm, gs_hbm, gate_hbm, up_hbm, cot_hbm,
    gx_hbm, gres_hbm, mixed_hbm, kept_hbm, given_hbm,
    tok_ref, normed_ref, wt_ref, gs_ref, gate_ref, up_ref, cot_ref,
    gx_ref, gres_ref, mixed_ref, gin_s, inner_ref, hs_ref, terms_s, term_s, in_sems, out_sems,
):
    pairs = (
        (tok_hbm, tok_ref), (normed_hbm, normed_ref), (wt_hbm, wt_ref),
        (gs_hbm, gs_ref), (gate_hbm, gate_ref), (up_hbm, up_ref), (cot_hbm, cot_ref),
    )
    def load(i, part):
        source, target = pairs[i]
        return pltpu.make_async_copy(source.at[part], target.at[part], in_sems.at[i, part.start // 4])

    rows_loads = [load(i, slice(0, pairs[i][1].shape[0])) for i in (0, 1, 6)]
    block_loads = [[load(i, part) for i in (2, 3, 4, 5)] for part in (slice(0, 4), slice(4, 8))]
    for copy in rows_loads[:2] + block_loads[0] + block_loads[1] + rows_loads[2:]:
        copy.start()
    for copy in rows_loads[:2]:
        copy.wait()
    mixed = from_chunks(mixx_ref[...])
    opened = sigmoid(normed_ref[...].astype(F32) * scale_ref[...] + bias_ref[...])
    resid = (tok_ref[...].astype(F32) + mixed * opened).astype(BF).astype(F32)
    inverse = inverse_rms(resid)
    inner_ref[...] = (resid * inverse * gain_ref[...]).astype(BF)
    mixed_ref[...] = mixed.astype(BF)
    store_mixed = pltpu.make_async_copy(mixed_ref, mixed_hbm, out_sems.at[0])
    store_mixed.start()

    def keep(which, k, term):
        zh, core, part = k >> 2, (k >> 1) & 1, k & 1
        for y in range(4):
            for x in range(4):
                start = y * 128 + x * 32
                terms_s[core, x, which, zh, part, y] = term[start : start + 32]

    for k in range(MB):
        if k in (0, 4):
            for copy in block_loads[k // 4]:
                copy.wait()
        inner = inner_ref[:, k * DB : (k + 1) * DB]
        pre = nt(wt_ref[k], inner)
        pre_gate = pre[:HB]
        pre_up = pre[HB:]
        sig = sigmoid(pre_gate)
        silu = pre_gate * sig
        g_hidden = gs_ref[k].astype(F32)
        hidden = (silu * pre_up).astype(BF)
        for kb in range(MB):
            hs_ref[kb, k * 64 : (k + 1) * 64, :] = hidden[kb * 64 : (kb + 1) * 64]
        g_gate = (g_hidden * pre_up * (sig + silu * (1.0 - sig))).astype(BF)
        g_up = (g_hidden * silu).astype(BF)
        keep(0, k, nn(g_gate, inner).astype(BF))
        keep(1, k, nn(g_up, inner).astype(BF))
        g_inner = nn(gate_ref[k], g_gate) + nn(up_ref[k], g_up)
        gin_s[:, k * DB : (k + 1) * DB] = g_inner.T
    core, x = place_ref[0], place_ref[1]
    stores = [store_mixed]

    def send(first, last):
        for which_core, target in ((1 - core, given_hbm), (core, kept_hbm)):
            for step in range(4):
                source = terms_s.at[which_core, (x + step) & 3, first:last]
                sem = out_sems.at[len(stores)]
                copy = pltpu.make_async_copy(source, target.at[step, first:last], sem)
                copy.start()
                stores.append(copy)

    send(0, 2)
    rows_loads[2].wait()
    for kb in range(MB):
        zh, half, part = kb >> 2, (kb >> 1) & 1, kb & 1
        term_s[kb] = nn(hs_ref[kb], cot_ref[:, kb * DB : (kb + 1) * DB])
        for y in range(4):
            for place in range(4):
                start = y * 16 + place * 4
                rows = [term_s[kb, pl.ds(start + j, 8, stride=64), :] for j in range(4)]
                terms_s[half, place, 2, zh, part, y] = jnp.concatenate(rows, axis=0).astype(BF)
    send(2, 3)
    for half in range(2):
        rows = slice(half * 128, half * 128 + 128)
        d_norm = gin_s[rows] * gain_ref[...]
        norm2 = resid[rows] * inverse[rows]
        average = jnp.mean(d_norm * norm2, axis=-1, keepdims=True)
        back = inverse[rows] * (d_norm - norm2 * average)
        g_resid = (cot_ref[rows].astype(F32) + back).astype(BF)
        gres_ref[rows] = g_resid
        chunk_rows = slice(half * 256, half * 256 + 256)
        gx_ref[chunk_rows] = to_chunks((g_resid.astype(F32) * opened[rows]).astype(BF))
        pairs = ((gx_ref.at[chunk_rows], gx_hbm.at[chunk_rows]), (gres_ref.at[rows], gres_hbm.at[rows]))
        for i, (source, target) in enumerate(pairs):
            stores.append(pltpu.make_async_copy(source, target, out_sems.at[17 + 2 * half + i]))
            stores[-1].start()
    for store in stores:
        store.wait()


def sum_core(kept_ref, got_ref, p0_ref, p1_ref, p2a_ref, p2b_ref, p3_ref):
    for step, out in ((0, p0_ref), (1, p1_ref), (3, p3_ref)):
        out[...] = (kept_ref[step].astype(F32) + got_ref[step].astype(F32)).astype(BF)
    for zh, out in ((0, p2a_ref), (1, p2b_ref)):
        out[...] = (kept_ref[2, :, zh].astype(F32) + got_ref[2, :, zh].astype(F32)).astype(BF)


def pass_on(p1_ref, p3_ref, p2a_ref, p2b_ref, up_ref, down_ref):
    up_ref[:, 0] = (p1_ref[:, 0].astype(F32) + p2a_ref[...].astype(F32)).astype(BF)
    up_ref[:, 1] = p1_ref[:, 1]
    down_ref[:, 0] = p3_ref[:, 0]
    down_ref[:, 1] = (p3_ref[:, 1].astype(F32) + p2b_ref[...].astype(F32)).astype(BF)


def sum_x(y_ref, *refs):
    pieces, outs = refs[:3], refs[3:]
    for step, out in enumerate(outs):
        y = (y_ref[0] + step) & 3
        total = pieces[0][:, :, :, y].astype(F32)
        for piece in pieces[1:]:
            total = total + piece[:, :, :, y].astype(F32)
        out[...] = total.astype(BF)


def sum_y(z_ref, *refs):
    gots, outs, total_s = refs[:4], refs[4:8], refs[8]
    total = gots[0][...].astype(F32)
    for got in gots[1:]:
        total = total + got[...].astype(F32)
    total_s[...] = total
    for step, out in enumerate(outs):
        zl = (z_ref[0] + step) & 3
        out[...] = total_s[:, :, :, pl.ds(pl.multiple_of(zl * 8, 8), 8), :]


def first_grad(dp_ref, gsx_ref, normed_ref, second_ref, gsec_ref, *refs):
    outs, terms = refs[:4], refs[4]
    gsec = from_chunks(gsx_ref[...]).astype(BF)
    gsec_ref[...] = gsec
    first = nt(normed_ref[...], gsec).astype(BF)
    for dp in range(4):
        terms[dp, 0:64, :] = first[dp * 64 : (dp + 1) * 64]
        terms[dp, 64:80, :] = second_ref[dp * 16 : (dp + 1) * 16, :]
    for step, out in enumerate(outs):
        out[...] = terms[dp_ref[0] ^ step]


def sum_z(zh_ref, *refs):
    lines, outs = refs[:4], refs[4:]
    for step, out in enumerate(outs):
        zh = zh_ref[0] ^ step
        total = lines[0][:, zh]
        for ref in lines[1:]:
            total = total + ref[:, zh]
        out[...] = total


def finish(
    gsec_ref, first_ref, tok_ref, gres_ref, mixed_ref, normed_ref, scale_ref, bias_ref, gain_ref,
    out_ref,
):
    scale = scale_ref[...]
    g_resid = gres_ref[...].astype(F32)
    opened = sigmoid(normed_ref[...].astype(F32) * scale + bias_ref[...])
    g_open = g_resid * mixed_ref[...].astype(F32) * opened * (1.0 - opened)
    d_norm = (tn(first_ref[...], gsec_ref[...]) + g_open * scale) * gain_ref[...]
    wide = tok_ref[...].astype(F32)
    inverse = inverse_rms(wide)
    normed = wide * inverse
    back = inverse * (d_norm - normed * jnp.mean(d_norm * normed, axis=-1, keepdims=True))
    out_ref[...] = (g_resid + back).astype(BF)


def call(kernel, outs, flops, scratch=(), vmem=58, scalars=0, manual=0, hbm_outs=0):
    def run(*args):
        vmem_spec = pl.BlockSpec(memory_space=pltpu.VMEM)
        any_spec = pl.BlockSpec(memory_space=pl.ANY)
        specs = [vmem_spec] * (len(args) - scalars - manual) + [any_spec] * manual
        specs = [pl.BlockSpec(memory_space=pltpu.SMEM)] * scalars + specs
        out_specs = [vmem_spec] * (len(outs) - hbm_outs) + [any_spec] * hbm_outs
        moved = sum(a.size * a.dtype.itemsize for a in args)
        moved += sum(o.size * o.dtype.itemsize for o in outs)
        return pl.pallas_call(
            kernel,
            out_shape=outs if len(outs) > 1 else outs[0],
            in_specs=specs,
            out_specs=out_specs if len(outs) > 1 else out_specs[0],
            scratch_shapes=scratch,
            compiler_params=pltpu.CompilerParams(vmem_limit_bytes=vmem * 2**20),
            cost_estimate=pl.CostEstimate(flops=flops, bytes_accessed=moved, transcendentals=0),
            name=kernel.__name__,
        )(*args)

    return run


def struct(shape, dtype=BF):
    return jax.ShapeDtypeStruct(shape, dtype)


def exchange(chunked, axis_names):
    return lax.all_to_all(chunked, axis_names, 0, 0, tiled=True)


def seq_exchange(value):
    return exchange(value.reshape(CHUNKS, 8, HALF), SEQ).reshape(HALF, HALF)


def index_of(axis_names):
    return lax.axis_index(axis_names).astype(jnp.int32).reshape(1)


def shift(value, axis_name, step):
    return lax.ppermute(value, axis_name, [(i, (i + step) % 4) for i in range(4)])


def body(
    tokens, cotangent, first_factor, second_factor, norm_gain, gate_scale, gate_bias,
    mlp_gain, gate_weight, up_weight, down_weight,
):
    tok = tokens.reshape(ROWS, WIDTH)
    cot = cotangent.reshape(ROWS, WIDTH)
    first = first_factor.reshape(ROWS, ROWS)
    second = second_factor.reshape(ROWS, CHUNKS)
    gain1 = norm_gain.reshape(1, WIDTH)
    scale = gate_scale.reshape(1, WIDTH)
    bias = gate_bias.reshape(1, WIDTH)
    gain2 = mlp_gain.reshape(1, WIDTH)
    square = struct((HALF, HALF))

    normed, sec = call(norm_section, (struct((ROWS, WIDTH)), square), 10**9)(tok, first, gain1)
    m = call(prepare_mix, (square,), 10**8, vmem=12)(second)
    sec_cols = seq_exchange(sec)
    mixed_cols = call(mix, (square,), 3 * 10**8, vmem=12)(m, sec_cols)
    down, mixed_cols = lax.optimization_barrier((down_weight, mixed_cols))
    mixx = seq_exchange(mixed_cols)
    wt, gs = call(
        prepare_mlp, (struct((MB, 2 * HB, DB)), struct((MB, HB, ROWS))), 2 * 10**9
    )(gate_weight, up_weight, down, cot)
    pieces_shape = struct((4, 3, 2, 2, 4, 32, DB))
    gmix, g_resid, mixed, kept, given = call(
        mlp,
        (square, struct((ROWS, WIDTH)), struct((ROWS, WIDTH)), pieces_shape, pieces_shape),
        6 * 10**9,
        scratch=[
            pltpu.VMEM((ROWS, WIDTH), BF),
            pltpu.VMEM((ROWS, WIDTH), BF),
            pltpu.VMEM((MB, 2 * HB, DB), BF),
            pltpu.VMEM((MB, HB, ROWS), BF),
            pltpu.VMEM((MB, DB, HB), BF),
            pltpu.VMEM((MB, DB, HB), BF),
            pltpu.VMEM((ROWS, WIDTH), BF),
            pltpu.VMEM((HALF, HALF), BF),
            pltpu.VMEM((ROWS, WIDTH), BF),
            pltpu.VMEM((ROWS, WIDTH), BF),
            pltpu.VMEM((ROWS, WIDTH), F32),
            pltpu.VMEM((ROWS, WIDTH), BF),
            pltpu.VMEM((MB, HB, ROWS), BF),
            pltpu.VMEM((2, 4, 3, 2, 2, 4, 32, DB), BF),
            pltpu.VMEM((MB, HB, DB), F32),
            pltpu.SemaphoreType.DMA((7, 2)),
            pltpu.SemaphoreType.DMA((21,)),
        ],
        scalars=1,
        manual=7,
        hbm_outs=5,
    )(
        jnp.concatenate([index_of("core"), index_of("x")]), scale, bias, gain2,
        mixx, tok, normed, wt, gs, gate_weight, up_weight, cot,
    )

    gmix_cols = seq_exchange(gmix)
    got = lax.ppermute(given, "core", [(0, 1), (1, 0)])
    piece, half = struct((3, 2, 2, 4, 32, DB)), struct((3, 2, 4, 32, DB))
    pieces = call(sum_core, (piece, piece, half, half, piece), 10**6, vmem=12)(kept, got)
    own, up, far_up, far_down, down = pieces
    far_up, far_down = shift(far_up, "x", 1), shift(far_down, "x", 3)
    up, down = call(pass_on, (piece, piece), 10**6, vmem=12)(up, down, far_up, far_down)
    gmix_cols, up, down = lax.optimization_barrier((gmix_cols, up, down))
    gsec_cols = call(mix_back, (square,), 4 * 10**8, vmem=12)(second, gmix_cols)
    gsx = seq_exchange(gsec_cols)
    up, down = shift(up, "x", 1), shift(down, "x", 3)
    rows = call(sum_x, (struct((3, 2, 2, 32, DB)),) * 4, SUM_X_COST, vmem=12, scalars=1)(
        index_of("y"), own, up, down
    )
    gots = [shift(rows[step], "y", step) for step in (1, 2, 3)]
    parts = call(
        sum_y,
        (struct((3, 2, 2, 8, DB), F32),) * 4,
        10**6,
        scratch=[pltpu.VMEM((3, 2, 2, 32, DB), F32)],
        scalars=1,
        vmem=12,
    )(index_of("zl"), rows[0], *gots)
    line = [parts[0]] + [shift(parts[step], "zl", step) for step in (1, 2, 3)]
    second_t = call(second_grad, (struct((CHUNKS, ROWS)),), 5 * 10**8, vmem=12)(
        sec_cols, gmix_cols
    )
    gsec, *terms = call(
        first_grad,
        (struct((ROWS, WIDTH)),) + (struct((80, ROWS)),) * 4,
        5 * 10**8,
        scratch=[pltpu.VMEM((4, 80, ROWS), BF)],
        scalars=1,
    )(index_of(DP), gsx, normed, second_t)
    grad_inputs = call(finish, (struct((ROWS, WIDTH)),), 2 * 10**8)(
        gsec, first, tok, g_resid, mixed, normed, scale, bias, gain1
    )

    total = terms[0].astype(F32)
    for step in (1, 2, 3):
        sent = lax.ppermute(terms[step], DP, [(i, i ^ step) for i in range(4)])
        total = total + sent.astype(F32)
    total = total * (4 * WIDTH) ** (-0.5)
    line = lax.optimization_barrier((line, terms[0]))[0]
    own, other = call(sum_z, (struct((3, 2, 8, DB), F32),) * 2, 10**6, scalars=1, vmem=12)(
        index_of("zh"), *line
    )
    whole = own + lax.ppermute(other, "zh", [(0, 1), (1, 0)])
    whole = (whole * (4 * ROWS * CHUNKS) ** (-0.5)).transpose(0, 1, 3, 2)
    return (
        grad_inputs[None],
        total[:64].T[None],
        total[64:].T.reshape(CHUNKS, 4, 16),
        whole[0],
        whole[1],
        whole[2],
    )


def solution(mesh):
    fine = Mesh(mesh.devices.reshape(2, 2, 4, 4, 4), ("zh", "core", "y", "x", "zl"))
    placed = (
        P(DP, SEQ, None),
        P(DP, SEQ, None),
        P(SEQ, None, None),
        P(None, SEQ, None),
    ) + (P(),) * 7
    return jax.shard_map(
        body,
        mesh=fine,
        in_specs=placed,
        out_specs=(
            P(DP, SEQ, None),
            P(SEQ, None, DP),
            P(None, SEQ, DP),
            P(DP, None, SEQ),
            P(DP, None, SEQ),
            P(DP, None, SEQ),
        ),
        check_vma=False,
    )
```

```python
import functools

import jax
import jax.numpy as jnp
from jax import lax
from jax.experimental import pallas as pl
from jax.experimental.pallas import tpu as pltpu
from jax.sharding import Mesh, PartitionSpec as P

EPS = 1e-05
VM = 63
SUM_X_COST = 2 * 10**10
BF = jnp.bfloat16
F32 = jnp.float32
SEQ = ("y", "x", "zl")
DP = ("zh", "core")

ROWS = 256
WIDTH = 1024
HALF = 512
CHUNKS = 64
MB = 8
HB = 512
DB = 128


def iota(shape, dim):
    return lax.broadcasted_iota(jnp.int32, shape, dim)


def one_hot(condition):
    return jnp.where(condition, 1.0, 0.0).astype(BF)


def nn(a, b):
    return jnp.dot(a, b, preferred_element_type=F32)


def nt(a, b):
    return lax.dot_general(a, b, (((1,), (1,)), ((), ())), preferred_element_type=F32)


def tn(a, b):
    return lax.dot_general(a, b, (((0,), (0,)), ((), ())), preferred_element_type=F32)


def to_chunks(value):
    row = iota((ROWS, ROWS), 0)
    col = iota((ROWS, ROWS), 1)
    perm = one_hot(col == (row & 4) * 32 + (row >> 3) * 4 + (row & 3))
    blocks = []
    for start in range(0, value.shape[0], 128):
        rows = value[start : start + 128]
        stacked = jnp.concatenate([rows[:, :HALF], rows[:, HALF:]], axis=0)
        blocks.append(nn(perm, stacked).astype(BF))
    return jnp.concatenate(blocks, axis=0)


def from_chunks(chunked):
    row = iota((ROWS, ROWS), 0)
    col = iota((ROWS, ROWS), 1)
    perm = one_hot(col == ((row >> 2) & 31) * 8 + (row >> 7) * 4 + (row & 3))
    blocks = []
    for start in range(0, chunked.shape[0], 256):
        stacked = nn(perm, chunked[start : start + 256])
        blocks.append(jnp.concatenate([stacked[:128], stacked[128:]], axis=1))
    return jnp.concatenate(blocks, axis=0)


def sigmoid(value):
    return 0.5 * jnp.tanh(0.5 * value) + 0.5


def inverse_rms(values):
    return lax.rsqrt(jnp.mean(values * values, axis=-1, keepdims=True) + EPS)


def norm_section(tok_ref, first_ref, gain_ref, normed_ref, sec_ref):
    wide = tok_ref[...].astype(F32)
    normed = (wide * inverse_rms(wide) * gain_ref[...]).astype(BF)
    normed_ref[...] = normed
    sec_ref[...] = to_chunks(nn(first_ref[...], normed).astype(BF))


def spread_rows():
    row = iota((HALF, ROWS), 0)
    col = iota((HALF, ROWS), 1)
    return one_hot(col == (row >> 3) * 4 + (row & 3))


def block_mask():
    return (iota((HALF, HALF), 0) & 7) == (iota((HALF, HALF), 1) & 7)


def block_of():
    return one_hot((iota((HALF, CHUNKS), 0) >> 3) == iota((HALF, CHUNKS), 1))


def prepare_mix(second_ref, m_ref):
    tall = nn(spread_rows(), second_ref[...]).astype(BF)
    m_ref[...] = jnp.where(block_mask(), nt(tall, block_of()), 0.0).astype(BF)


def mix_back(second_ref, x_ref, out_ref):
    tall = nt(block_of(), second_ref[...]).astype(BF)
    back = jnp.where(block_mask(), nt(tall, spread_rows()), 0.0).astype(BF)
    out_ref[...] = nn(back, x_ref[...]).astype(BF)


def prepare_mlp(gate_ref, up_ref, down_ref, cot_ref, wt_ref, gs_ref):
    row = iota((HB, HB), 0)
    col = iota((HB, HB), 1)
    same = one_hot(row == col)
    regroup = one_hot(col == (row & 63) * 8 + (row >> 6))
    for k in range(MB):
        wt_ref[k, 0:HB, :] = nt(same, gate_ref[k]).astype(BF)
        wt_ref[k, HB:, :] = nt(same, up_ref[k]).astype(BF)
    for kb in range(MB):
        down = nt(regroup, down_ref[kb]).astype(BF)
        g_perm = nt(down, cot_ref[:, kb * DB : (kb + 1) * DB]).astype(BF)
        for k in range(MB):
            gs_ref[k, kb * 64 : (kb + 1) * 64, :] = g_perm[k * 64 : (k + 1) * 64]


def mix(m_ref, x_ref, out_ref):
    out_ref[...] = nn(m_ref[...], x_ref[...]).astype(BF)


def second_grad(sec_ref, gmix_ref, out_ref):
    pairs = nt(sec_ref[...], gmix_ref[...])
    pairs = jnp.where(block_mask(), pairs, 0.0).astype(BF)
    gather = one_hot(iota((CHUNKS, HALF), 0) == (iota((CHUNKS, HALF), 1) >> 3))
    picked = nn(gather, pairs).astype(BF)
    out_ref[...] = nn(picked, spread_rows()).astype(BF)


def mlp(
    place_ref, scale_ref, bias_ref, gain_ref,
    mixx_hbm, tok_hbm, normed_hbm, wt_hbm, gs_hbm, gate_hbm, up_hbm, cot_hbm,
    gx_hbm, gres_hbm, mixed_hbm, kept_hbm, given_hbm,
    mixx_ref, tok_ref, normed_ref, wt_ref, gs_ref, gate_ref, up_ref, cot_ref,
    gx_ref, gres_ref, mixed_ref, gin_s, inner_ref, hs_ref, terms_s, term_s, in_sems, out_sems,
):
    pairs = (
        (mixx_hbm, mixx_ref), (tok_hbm, tok_ref), (normed_hbm, normed_ref), (wt_hbm, wt_ref),
        (gs_hbm, gs_ref), (gate_hbm, gate_ref), (up_hbm, up_ref), (cot_hbm, cot_ref),
    )
    def load(i, part):
        source, target = pairs[i]
        return pltpu.make_async_copy(source.at[part], target.at[part], in_sems.at[i, part.start // 4])

    rows_loads = [load(i, slice(0, pairs[i][1].shape[0])) for i in (0, 1, 2, 7)]
    block_loads = [[load(i, part) for i in (3, 4, 5, 6)] for part in (slice(0, 4), slice(4, 8))]
    for copy in rows_loads[:3] + block_loads[0] + block_loads[1] + rows_loads[3:]:
        copy.start()
    for copy in rows_loads[:3]:
        copy.wait()
    mixed = from_chunks(mixx_ref[...])
    opened = sigmoid(normed_ref[...].astype(F32) * scale_ref[...] + bias_ref[...])
    resid = (tok_ref[...].astype(F32) + mixed * opened).astype(BF).astype(F32)
    inverse = inverse_rms(resid)
    inner_ref[...] = (resid * inverse * gain_ref[...]).astype(BF)
    mixed_ref[...] = mixed.astype(BF)
    store_mixed = pltpu.make_async_copy(mixed_ref, mixed_hbm, out_sems.at[0])
    store_mixed.start()

    def keep(which, k, term):
        zh, core, part = k >> 2, (k >> 1) & 1, k & 1
        for y in range(4):
            for x in range(4):
                start = y * 128 + x * 32
                terms_s[core, x, which, zh, part, y] = term[start : start + 32]

    for k in range(MB):
        if k in (0, 4):
            for copy in block_loads[k // 4]:
                copy.wait()
        inner = inner_ref[:, k * DB : (k + 1) * DB]
        pre = nt(wt_ref[k], inner)
        pre_gate = pre[:HB]
        pre_up = pre[HB:]
        sig = sigmoid(pre_gate)
        silu = pre_gate * sig
        g_hidden = gs_ref[k].astype(F32)
        hidden = (silu * pre_up).astype(BF)
        for kb in range(MB):
            hs_ref[kb, k * 64 : (k + 1) * 64, :] = hidden[kb * 64 : (kb + 1) * 64]
        g_gate = (g_hidden * pre_up * (sig + silu * (1.0 - sig))).astype(BF)
        g_up = (g_hidden * silu).astype(BF)
        keep(0, k, nn(g_gate, inner).astype(BF))
        keep(1, k, nn(g_up, inner).astype(BF))
        g_inner = nn(gate_ref[k], g_gate) + nn(up_ref[k], g_up)
        gin_s[:, k * DB : (k + 1) * DB] = g_inner.T
    core, x = place_ref[0], place_ref[1]
    stores = [store_mixed]

    def send(first, last):
        for which_core, target in ((1 - core, given_hbm), (core, kept_hbm)):
            for step in range(4):
                source = terms_s.at[which_core, (x + step) & 3, first:last]
                sem = out_sems.at[len(stores)]
                copy = pltpu.make_async_copy(source, target.at[step, first:last], sem)
                copy.start()
                stores.append(copy)

    send(0, 2)
    rows_loads[3].wait()
    for kb in range(MB):
        zh, half, part = kb >> 2, (kb >> 1) & 1, kb & 1
        term_s[kb] = nn(hs_ref[kb], cot_ref[:, kb * DB : (kb + 1) * DB])
        for y in range(4):
            for place in range(4):
                start = y * 16 + place * 4
                rows = [term_s[kb, pl.ds(start + j, 8, stride=64), :] for j in range(4)]
                terms_s[half, place, 2, zh, part, y] = jnp.concatenate(rows, axis=0).astype(BF)
    send(2, 3)
    for half in range(2):
        rows = slice(half * 128, half * 128 + 128)
        d_norm = gin_s[rows] * gain_ref[...]
        norm2 = resid[rows] * inverse[rows]
        average = jnp.mean(d_norm * norm2, axis=-1, keepdims=True)
        back = inverse[rows] * (d_norm - norm2 * average)
        g_resid = (cot_ref[rows].astype(F32) + back).astype(BF)
        gres_ref[rows] = g_resid
        chunk_rows = slice(half * 256, half * 256 + 256)
        gx_ref[chunk_rows] = to_chunks((g_resid.astype(F32) * opened[rows]).astype(BF))
        pairs = ((gx_ref.at[chunk_rows], gx_hbm.at[chunk_rows]), (gres_ref.at[rows], gres_hbm.at[rows]))
        for i, (source, target) in enumerate(pairs):
            stores.append(pltpu.make_async_copy(source, target, out_sems.at[17 + 2 * half + i]))
            stores[-1].start()
    for store in stores:
        store.wait()


def sum_core(kept_ref, got_ref, p0_ref, p1_ref, p2a_ref, p2b_ref, p3_ref):
    for step, out in ((0, p0_ref), (1, p1_ref), (3, p3_ref)):
        out[...] = (kept_ref[step].astype(F32) + got_ref[step].astype(F32)).astype(BF)
    for zh, out in ((0, p2a_ref), (1, p2b_ref)):
        out[...] = (kept_ref[2, :, zh].astype(F32) + got_ref[2, :, zh].astype(F32)).astype(BF)


def pass_on(p1_ref, p3_ref, p2a_ref, p2b_ref, up_ref, down_ref):
    up_ref[:, 0] = (p1_ref[:, 0].astype(F32) + p2a_ref[...].astype(F32)).astype(BF)
    up_ref[:, 1] = p1_ref[:, 1]
    down_ref[:, 0] = p3_ref[:, 0]
    down_ref[:, 1] = (p3_ref[:, 1].astype(F32) + p2b_ref[...].astype(F32)).astype(BF)


def sum_x(y_ref, *refs):
    pieces, outs = refs[:3], refs[3:]
    for step, out in enumerate(outs):
        y = (y_ref[0] + step) & 3
        total = pieces[0][:, :, :, y].astype(F32)
        for piece in pieces[1:]:
            total = total + piece[:, :, :, y].astype(F32)
        out[...] = total.astype(BF)


def sum_y(z_ref, *refs):
    gots, outs, total_s = refs[:4], refs[4:8], refs[8]
    total = gots[0][...].astype(F32)
    for got in gots[1:]:
        total = total + got[...].astype(F32)
    total_s[...] = total
    for step, out in enumerate(outs):
        zl = (z_ref[0] + step) & 3
        out[...] = total_s[:, :, :, pl.ds(pl.multiple_of(zl * 8, 8), 8), :]


def first_grad(dp_ref, gsx_ref, normed_ref, second_ref, gsec_ref, kept_ref, *refs):
    given_refs, terms = refs[:2], refs[2]
    gsec = from_chunks(gsx_ref[...]).astype(BF)
    gsec_ref[...] = gsec
    first = nt(normed_ref[...], gsec).astype(BF)
    for dp in range(4):
        terms[dp, 0:64, :] = first[dp * 64 : (dp + 1) * 64]
        terms[dp, 64:80, :] = second_ref[dp * 16 : (dp + 1) * 16, :]
    for step in range(2):
        kept_ref[step] = terms[dp_ref[0] ^ (2 * step)]
        given_refs[step][...] = terms[dp_ref[0] ^ (2 * step + 1)]


def sum_pair(zh_ref, kept_ref, got0_ref, got1_ref, *refs):
    lines, own_ref, own_line_ref, sent_ref = refs[:4], refs[4], refs[5], refs[6]

    def line_sum(zh):
        total = lines[0][:, zh]
        for ref in lines[1:]:
            total = total + ref[:, zh]
        return total.reshape(48, DB)

    own_ref[...] = kept_ref[0].astype(F32) + got0_ref[...].astype(F32)
    own_line_ref[...] = line_sum(zh_ref[0])
    sent_ref[0:80, :] = (kept_ref[1].astype(F32) + got1_ref[...].astype(F32)).astype(BF)
    other = line_sum(1 - zh_ref[0])
    padded = jnp.concatenate([other[32:], jnp.zeros((16, DB), F32)], axis=0)
    sent_ref[80:112, :] = jnp.concatenate([other[:32], padded], axis=1).astype(BF)


def finish(
    gsec_ref, first_ref, tok_ref, gres_ref, mixed_ref, normed_ref, scale_ref, bias_ref, gain_ref,
    out_ref,
):
    scale = scale_ref[...]
    g_resid = gres_ref[...].astype(F32)
    opened = sigmoid(normed_ref[...].astype(F32) * scale + bias_ref[...])
    g_open = g_resid * mixed_ref[...].astype(F32) * opened * (1.0 - opened)
    d_norm = (tn(first_ref[...], gsec_ref[...]) + g_open * scale) * gain_ref[...]
    wide = tok_ref[...].astype(F32)
    inverse = inverse_rms(wide)
    normed = wide * inverse
    back = inverse * (d_norm - normed * jnp.mean(d_norm * normed, axis=-1, keepdims=True))
    out_ref[...] = (g_resid + back).astype(BF)


def call(kernel, outs, flops, scratch=(), vmem=58, scalars=0, manual=0, hbm_outs=0):
    def run(*args):
        vmem_spec = pl.BlockSpec(memory_space=pltpu.VMEM)
        any_spec = pl.BlockSpec(memory_space=pl.ANY)
        specs = [vmem_spec] * (len(args) - scalars - manual) + [any_spec] * manual
        specs = [pl.BlockSpec(memory_space=pltpu.SMEM)] * scalars + specs
        out_specs = [vmem_spec] * (len(outs) - hbm_outs) + [any_spec] * hbm_outs
        moved = sum(a.size * a.dtype.itemsize for a in args)
        moved += sum(o.size * o.dtype.itemsize for o in outs)
        return pl.pallas_call(
            kernel,
            out_shape=outs if len(outs) > 1 else outs[0],
            in_specs=specs,
            out_specs=out_specs if len(outs) > 1 else out_specs[0],
            scratch_shapes=scratch,
            compiler_params=pltpu.CompilerParams(vmem_limit_bytes=vmem * 2**20),
            cost_estimate=pl.CostEstimate(flops=flops, bytes_accessed=moved, transcendentals=0),
            name=kernel.__name__,
        )(*args)

    return run


def struct(shape, dtype=BF):
    return jax.ShapeDtypeStruct(shape, dtype)


def exchange(chunked, axis_names):
    return lax.all_to_all(chunked, axis_names, 0, 0, tiled=True)


def seq_exchange(value):
    return exchange(value.reshape(CHUNKS, 8, HALF), SEQ).reshape(HALF, HALF)


def index_of(axis_names):
    return lax.axis_index(axis_names).astype(jnp.int32).reshape(1)


def shift(value, axis_name, step):
    return lax.ppermute(value, axis_name, [(i, (i + step) % 4) for i in range(4)])


def body(
    tokens, cotangent, first_factor, second_factor, norm_gain, gate_scale, gate_bias,
    mlp_gain, gate_weight, up_weight, down_weight,
):
    tok = tokens.reshape(ROWS, WIDTH)
    cot = cotangent.reshape(ROWS, WIDTH)
    first = first_factor.reshape(ROWS, ROWS)
    second = second_factor.reshape(ROWS, CHUNKS)
    gain1 = norm_gain.reshape(1, WIDTH)
    scale = gate_scale.reshape(1, WIDTH)
    bias = gate_bias.reshape(1, WIDTH)
    gain2 = mlp_gain.reshape(1, WIDTH)
    square = struct((HALF, HALF))

    normed, sec = call(norm_section, (struct((ROWS, WIDTH)), square), 10**9)(tok, first, gain1)
    m = call(prepare_mix, (square,), 10**8, vmem=12)(second)
    sec_cols = seq_exchange(sec)
    mixed_cols = call(mix, (square,), 3 * 10**8, vmem=12)(m, sec_cols)
    down, mixed_cols = lax.optimization_barrier((down_weight, mixed_cols))
    mixx = seq_exchange(mixed_cols)
    wt, gs = call(
        prepare_mlp, (struct((MB, 2 * HB, DB)), struct((MB, HB, ROWS))), 2 * 10**9, vmem=VM
    )(gate_weight, up_weight, down, cot)
    pieces_shape = struct((4, 3, 2, 2, 4, 32, DB))
    gmix, g_resid, mixed, kept, given = call(
        mlp,
        (square, struct((ROWS, WIDTH)), struct((ROWS, WIDTH)), pieces_shape, pieces_shape),
        6 * 10**9,
        scratch=[
            pltpu.VMEM((HALF, HALF), BF),
            pltpu.VMEM((ROWS, WIDTH), BF),
            pltpu.VMEM((ROWS, WIDTH), BF),
            pltpu.VMEM((MB, 2 * HB, DB), BF),
            pltpu.VMEM((MB, HB, ROWS), BF),
            pltpu.VMEM((MB, DB, HB), BF),
            pltpu.VMEM((MB, DB, HB), BF),
            pltpu.VMEM((ROWS, WIDTH), BF),
            pltpu.VMEM((HALF, HALF), BF),
            pltpu.VMEM((ROWS, WIDTH), BF),
            pltpu.VMEM((ROWS, WIDTH), BF),
            pltpu.VMEM((ROWS, WIDTH), F32),
            pltpu.VMEM((ROWS, WIDTH), BF),
            pltpu.VMEM((MB, HB, ROWS), BF),
            pltpu.VMEM((2, 4, 3, 2, 2, 4, 32, DB), BF),
            pltpu.VMEM((MB, HB, DB), F32),
            pltpu.SemaphoreType.DMA((8, 2)),
            pltpu.SemaphoreType.DMA((21,)),
        ],
        scalars=1,
        manual=8,
        hbm_outs=5,
        vmem=VM,
    )(
        jnp.concatenate([index_of("core"), index_of("x")]), scale, bias, gain2,
        mixx, tok, normed, wt, gs, gate_weight, up_weight, cot,
    )

    gmix_cols = seq_exchange(gmix)
    got = lax.ppermute(given, "core", [(0, 1), (1, 0)])
    piece, half = struct((3, 2, 2, 4, 32, DB)), struct((3, 2, 4, 32, DB))
    pieces = call(sum_core, (piece, piece, half, half, piece), 10**6, vmem=12)(kept, got)
    own, up, far_up, far_down, down = pieces
    far_up, far_down = shift(far_up, "x", 1), shift(far_down, "x", 3)
    up, down = call(pass_on, (piece, piece), 10**6, vmem=12)(up, down, far_up, far_down)
    gmix_cols, up, down = lax.optimization_barrier((gmix_cols, up, down))
    gsec_cols = call(mix_back, (square,), 4 * 10**8, vmem=12)(second, gmix_cols)
    gsx = seq_exchange(gsec_cols)
    up, down = shift(up, "x", 1), shift(down, "x", 3)
    rows = call(sum_x, (struct((3, 2, 2, 32, DB)),) * 4, SUM_X_COST, vmem=12, scalars=1)(
        index_of("y"), own, up, down
    )
    gots = [shift(rows[step], "y", step) for step in (1, 2, 3)]
    parts = call(
        sum_y,
        (struct((3, 2, 2, 8, DB), F32),) * 4,
        10**6,
        scratch=[pltpu.VMEM((3, 2, 2, 32, DB), F32)],
        scalars=1,
        vmem=12,
    )(index_of("zl"), rows[0], *gots)
    line = [parts[0]] + [shift(parts[step], "zl", step) for step in (1, 2, 3)]
    gsx = lax.optimization_barrier((gsx, parts[0]))[0]
    second_t = call(second_grad, (struct((CHUNKS, ROWS)),), 5 * 10**8, vmem=12)(
        sec_cols, gmix_cols
    )
    gsec, kept, *given = call(
        first_grad,
        (struct((ROWS, WIDTH)), struct((2, 80, ROWS))) + (struct((80, ROWS)),) * 2,
        5 * 10**8,
        scratch=[pltpu.VMEM((4, 80, ROWS), BF)],
        scalars=1,
    )(index_of(DP), gsx, normed, second_t)
    grad_inputs = call(finish, (struct((ROWS, WIDTH)),), 2 * 10**8)(
        gsec, first, tok, g_resid, mixed, normed, scale, bias, gain1
    )

    gots = [lax.ppermute(piece, "core", [(0, 1), (1, 0)]) for piece in given]
    own, own_line, sent = call(
        sum_pair,
        (struct((80, ROWS), F32), struct((48, DB), F32), struct((112, ROWS))),
        10**6,
        scalars=1,
        vmem=12,
    )(index_of("zh"), kept, *gots, *line)
    sent = lax.ppermute(sent, "zh", [(0, 1), (1, 0)]).astype(F32)
    total = (own + sent[:80]) * (4 * WIDTH) ** (-0.5)
    whole = own_line + jnp.concatenate([sent[80:, :DB], sent[80:96, DB:]], axis=0)
    whole = whole * (4 * ROWS * CHUNKS) ** (-0.5)
    whole = whole.reshape(3, 2, 8, DB).transpose(0, 1, 3, 2)
    return (
        grad_inputs[None],
        total[:64].T[None],
        total[64:].T.reshape(CHUNKS, 4, 16),
        whole[0],
        whole[1],
        whole[2],
    )


def solution(mesh):
    fine = Mesh(mesh.devices.reshape(2, 2, 4, 4, 4), ("zh", "core", "y", "x", "zl"))
    placed = (
        P(DP, SEQ, None),
        P(DP, SEQ, None),
        P(SEQ, None, None),
        P(None, SEQ, None),
    ) + (P(),) * 7
    return jax.shard_map(
        body,
        mesh=fine,
        in_specs=placed,
        out_specs=(
            P(DP, SEQ, None),
            P(SEQ, None, DP),
            P(None, SEQ, DP),
            P(DP, None, SEQ),
            P(DP, None, SEQ),
            P(DP, None, SEQ),
        ),
        check_vma=False,
    )
```

```python
import functools

import jax
import jax.numpy as jnp
from jax import lax
from jax.experimental import pallas as pl
from jax.experimental.pallas import tpu as pltpu
from jax.sharding import Mesh, PartitionSpec as P

EPS = 1e-05
VM = 63
SUM_X_COST = 2 * 10**10
BF = jnp.bfloat16
F32 = jnp.float32
SEQ = ("y", "x", "zl")
DP = ("zh", "core")

ROWS = 256
WIDTH = 1024
HALF = 512
CHUNKS = 64
MB = 8
HB = 512
DB = 128


def iota(shape, dim):
    return lax.broadcasted_iota(jnp.int32, shape, dim)


def one_hot(condition):
    return jnp.where(condition, 1.0, 0.0).astype(BF)


def nn(a, b):
    return jnp.dot(a, b, preferred_element_type=F32)


def nt(a, b):
    return lax.dot_general(a, b, (((1,), (1,)), ((), ())), preferred_element_type=F32)


def tn(a, b):
    return lax.dot_general(a, b, (((0,), (0,)), ((), ())), preferred_element_type=F32)


def to_chunks(value):
    row = iota((ROWS, ROWS), 0)
    col = iota((ROWS, ROWS), 1)
    perm = one_hot(col == (row & 4) * 32 + (row >> 3) * 4 + (row & 3))
    blocks = []
    for start in range(0, value.shape[0], 128):
        rows = value[start : start + 128]
        stacked = jnp.concatenate([rows[:, :HALF], rows[:, HALF:]], axis=0)
        blocks.append(nn(perm, stacked).astype(BF))
    return jnp.concatenate(blocks, axis=0)


def from_chunks(chunked):
    row = iota((ROWS, ROWS), 0)
    col = iota((ROWS, ROWS), 1)
    perm = one_hot(col == ((row >> 2) & 31) * 8 + (row >> 7) * 4 + (row & 3))
    blocks = []
    for start in range(0, chunked.shape[0], 256):
        stacked = nn(perm, chunked[start : start + 256])
        blocks.append(jnp.concatenate([stacked[:128], stacked[128:]], axis=1))
    return jnp.concatenate(blocks, axis=0)


def sigmoid(value):
    return 0.5 * jnp.tanh(0.5 * value) + 0.5


def inverse_rms(values):
    return lax.rsqrt(jnp.mean(values * values, axis=-1, keepdims=True) + EPS)


def norm_section(tok_ref, first_ref, gain_ref, normed_ref, sec_ref):
    wide = tok_ref[...].astype(F32)
    normed = (wide * inverse_rms(wide) * gain_ref[...]).astype(BF)
    normed_ref[...] = normed
    sec_ref[...] = to_chunks(nn(first_ref[...], normed).astype(BF))


def spread_rows():
    row = iota((HALF, ROWS), 0)
    col = iota((HALF, ROWS), 1)
    return one_hot(col == (row >> 3) * 4 + (row & 3))


def block_mask():
    return (iota((HALF, HALF), 0) & 7) == (iota((HALF, HALF), 1) & 7)


def block_of():
    return one_hot((iota((HALF, CHUNKS), 0) >> 3) == iota((HALF, CHUNKS), 1))


def prepare_mix(second_ref, m_ref):
    tall = nn(spread_rows(), second_ref[...]).astype(BF)
    m_ref[...] = jnp.where(block_mask(), nt(tall, block_of()), 0.0).astype(BF)


def mix_back(second_ref, x_ref, out_ref):
    tall = nt(block_of(), second_ref[...]).astype(BF)
    back = jnp.where(block_mask(), nt(tall, spread_rows()), 0.0).astype(BF)
    out_ref[...] = nn(back, x_ref[...]).astype(BF)


def prepare_mlp(gate_ref, up_ref, down_ref, cot_ref, wt_ref, gs_ref):
    row = iota((HB, HB), 0)
    col = iota((HB, HB), 1)
    same = one_hot(row == col)
    regroup = one_hot(col == (row & 63) * 8 + (row >> 6))
    for k in range(MB):
        wt_ref[k, 0:HB, :] = nt(same, gate_ref[k]).astype(BF)
        wt_ref[k, HB:, :] = nt(same, up_ref[k]).astype(BF)
    for kb in range(MB):
        down = nt(regroup, down_ref[kb]).astype(BF)
        g_perm = nt(down, cot_ref[:, kb * DB : (kb + 1) * DB]).astype(BF)
        for k in range(MB):
            gs_ref[k, kb * 64 : (kb + 1) * 64, :] = g_perm[k * 64 : (k + 1) * 64]


def mix(m_ref, x_ref, out_ref):
    out_ref[...] = nn(m_ref[...], x_ref[...]).astype(BF)


def second_grad(sec_ref, gmix_ref, out_ref):
    pairs = nt(sec_ref[...], gmix_ref[...])
    pairs = jnp.where(block_mask(), pairs, 0.0).astype(BF)
    gather = one_hot(iota((CHUNKS, HALF), 0) == (iota((CHUNKS, HALF), 1) >> 3))
    picked = nn(gather, pairs).astype(BF)
    out_ref[...] = nn(picked, spread_rows()).astype(BF)


def mlp(
    place_ref, scale_ref, bias_ref, gain_ref,
    mixx_hbm, tok_hbm, normed_hbm, wt_hbm, gs_hbm, gate_hbm, up_hbm, cot_hbm,
    gx_hbm, gres_hbm, mixed_hbm, kept_hbm, given0_hbm, given1_hbm, given2_hbm, given3_hbm,
    mixx_ref, tok_ref, normed_ref, wt_ref, gs_ref, gate_ref, up_ref, cot_ref,
    gx_ref, gres_ref, mixed_ref, gin_s, inner_ref, hs_ref, terms_s, term_s, in_sems, out_sems,
):
    pairs = (
        (mixx_hbm, mixx_ref), (tok_hbm, tok_ref), (normed_hbm, normed_ref), (wt_hbm, wt_ref),
        (gs_hbm, gs_ref), (gate_hbm, gate_ref), (up_hbm, up_ref), (cot_hbm, cot_ref),
    )
    def load(i, part):
        source, target = pairs[i]
        return pltpu.make_async_copy(source.at[part], target.at[part], in_sems.at[i, part.start // 4])

    rows_loads = [load(i, slice(0, pairs[i][1].shape[0])) for i in (0, 1, 2, 7)]
    block_loads = [[load(i, part) for i in (3, 4, 5, 6)] for part in (slice(0, 4), slice(4, 8))]
    for copy in rows_loads[:3] + block_loads[0] + block_loads[1] + rows_loads[3:]:
        copy.start()
    for copy in rows_loads[:3]:
        copy.wait()
    mixed = from_chunks(mixx_ref[...])
    opened = sigmoid(normed_ref[...].astype(F32) * scale_ref[...] + bias_ref[...])
    resid = (tok_ref[...].astype(F32) + mixed * opened).astype(BF).astype(F32)
    inverse = inverse_rms(resid)
    inner_ref[...] = (resid * inverse * gain_ref[...]).astype(BF)
    mixed_ref[...] = mixed.astype(BF)
    store_mixed = pltpu.make_async_copy(mixed_ref, mixed_hbm, out_sems.at[0])
    store_mixed.start()

    def keep(which, k, term):
        zh, core, part = k >> 2, (k >> 1) & 1, k & 1
        for y in range(4):
            for x in range(4):
                start = y * 128 + x * 32
                terms_s[core, x, which, zh, part, y] = term[start : start + 32]

    for k in range(MB):
        if k in (0, 4):
            for copy in block_loads[k // 4]:
                copy.wait()
        inner = inner_ref[:, k * DB : (k + 1) * DB]
        pre = nt(wt_ref[k], inner)
        pre_gate = pre[:HB]
        pre_up = pre[HB:]
        sig = sigmoid(pre_gate)
        silu = pre_gate * sig
        g_hidden = gs_ref[k].astype(F32)
        hidden = (silu * pre_up).astype(BF)
        for kb in range(MB):
            hs_ref[kb, k * 64 : (k + 1) * 64, :] = hidden[kb * 64 : (kb + 1) * 64]
        g_gate = (g_hidden * pre_up * (sig + silu * (1.0 - sig))).astype(BF)
        g_up = (g_hidden * silu).astype(BF)
        keep(0, k, nn(g_gate, inner).astype(BF))
        keep(1, k, nn(g_up, inner).astype(BF))
        g_inner = nn(gate_ref[k], g_gate) + nn(up_ref[k], g_up)
        gin_s[:, k * DB : (k + 1) * DB] = g_inner.T
    core, x = place_ref[0], place_ref[1]
    stores = [store_mixed]

    def send(first, last):
        givens = (given0_hbm, given1_hbm, given2_hbm, given3_hbm)
        kepts = [kept_hbm.at[step] for step in range(4)]
        for which_core, targets in ((1 - core, givens), (core, kepts)):
            for step in range(4):
                source = terms_s.at[which_core, (x + step) & 3, first:last]
                sem = out_sems.at[len(stores)]
                copy = pltpu.make_async_copy(source, targets[step].at[first:last], sem)
                copy.start()
                stores.append(copy)

    send(0, 2)
    rows_loads[3].wait()
    for kb in range(MB):
        zh, half, part = kb >> 2, (kb >> 1) & 1, kb & 1
        term_s[kb] = nn(hs_ref[kb], cot_ref[:, kb * DB : (kb + 1) * DB])
        for y in range(4):
            for place in range(4):
                start = y * 16 + place * 4
                rows = [term_s[kb, pl.ds(start + j, 8, stride=64), :] for j in range(4)]
                terms_s[half, place, 2, zh, part, y] = jnp.concatenate(rows, axis=0).astype(BF)
    send(2, 3)
    for half in range(2):
        rows = slice(half * 128, half * 128 + 128)
        d_norm = gin_s[rows] * gain_ref[...]
        norm2 = resid[rows] * inverse[rows]
        average = jnp.mean(d_norm * norm2, axis=-1, keepdims=True)
        back = inverse[rows] * (d_norm - norm2 * average)
        g_resid = (cot_ref[rows].astype(F32) + back).astype(BF)
        gres_ref[rows] = g_resid
        chunk_rows = slice(half * 256, half * 256 + 256)
        gx_ref[chunk_rows] = to_chunks((g_resid.astype(F32) * opened[rows]).astype(BF))
        pairs = ((gx_ref.at[chunk_rows], gx_hbm.at[chunk_rows]), (gres_ref.at[rows], gres_hbm.at[rows]))
        for i, (source, target) in enumerate(pairs):
            stores.append(pltpu.make_async_copy(source, target, out_sems.at[17 + 2 * half + i]))
            stores[-1].start()
    for store in stores:
        store.wait()


def sum_core(kept_ref, got0_ref, got1_ref, got2_ref, got3_ref, p0_ref, p1_ref, p2a_ref, p2b_ref, p3_ref):
    for step, got, out in ((0, got0_ref, p0_ref), (1, got1_ref, p1_ref), (3, got3_ref, p3_ref)):
        out[...] = (kept_ref[step].astype(F32) + got[...].astype(F32)).astype(BF)
    for zh, out in ((0, p2a_ref), (1, p2b_ref)):
        out[...] = (kept_ref[2, :, zh].astype(F32) + got2_ref[:, zh].astype(F32)).astype(BF)


def pass_on(p1_ref, p3_ref, p2a_ref, p2b_ref, up_ref, down_ref):
    up_ref[:, 0] = (p1_ref[:, 0].astype(F32) + p2a_ref[...].astype(F32)).astype(BF)
    up_ref[:, 1] = p1_ref[:, 1]
    down_ref[:, 0] = p3_ref[:, 0]
    down_ref[:, 1] = (p3_ref[:, 1].astype(F32) + p2b_ref[...].astype(F32)).astype(BF)


def sum_x(y_ref, *refs):
    pieces, outs = refs[:3], refs[3:]
    for step, out in enumerate(outs):
        y = (y_ref[0] + step) & 3
        total = pieces[0][:, :, :, y].astype(F32)
        for piece in pieces[1:]:
            total = total + piece[:, :, :, y].astype(F32)
        out[...] = total.astype(BF)


def sum_y(z_ref, *refs):
    gots, outs, total_s = refs[:4], refs[4:8], refs[8]
    total = gots[0][...].astype(F32)
    for got in gots[1:]:
        total = total + got[...].astype(F32)
    total_s[...] = total
    for step, out in enumerate(outs):
        zl = (z_ref[0] + step) & 3
        out[...] = total_s[:, :, :, pl.ds(pl.multiple_of(zl * 8, 8), 8), :]


def first_grad(dp_ref, gsx_ref, normed_ref, second_ref, gsec_ref, kept_ref, *refs):
    given_refs, terms = refs[:2], refs[2]
    gsec = from_chunks(gsx_ref[...]).astype(BF)
    gsec_ref[...] = gsec
    first = nt(normed_ref[...], gsec).astype(BF)
    for dp in range(4):
        terms[dp, 0:64, :] = first[dp * 64 : (dp + 1) * 64]
        terms[dp, 64:80, :] = second_ref[dp * 16 : (dp + 1) * 16, :]
    for step in range(2):
        kept_ref[step] = terms[dp_ref[0] ^ (2 * step)]
        given_refs[step][...] = terms[dp_ref[0] ^ (2 * step + 1)]


def sum_pair(zh_ref, kept_ref, got0_ref, got1_ref, *refs):
    lines, own_ref, own_line_ref, sent_ref = refs[:4], refs[4], refs[5], refs[6]

    def line_sum(zh):
        total = lines[0][:, zh]
        for ref in lines[1:]:
            total = total + ref[:, zh]
        return total.reshape(48, DB)

    own_ref[...] = kept_ref[0].astype(F32) + got0_ref[...].astype(F32)
    own_line_ref[...] = line_sum(zh_ref[0])
    sent_ref[0:80, :] = (kept_ref[1].astype(F32) + got1_ref[...].astype(F32)).astype(BF)
    other = line_sum(1 - zh_ref[0])
    padded = jnp.concatenate([other[32:], jnp.zeros((16, DB), F32)], axis=0)
    sent_ref[80:112, :] = jnp.concatenate([other[:32], padded], axis=1).astype(BF)


def finish(
    gsec_ref, first_ref, tok_ref, gres_ref, mixed_ref, normed_ref, scale_ref, bias_ref, gain_ref,
    out_ref,
):
    scale = scale_ref[...]
    g_resid = gres_ref[...].astype(F32)
    opened = sigmoid(normed_ref[...].astype(F32) * scale + bias_ref[...])
    g_open = g_resid * mixed_ref[...].astype(F32) * opened * (1.0 - opened)
    d_norm = (tn(first_ref[...], gsec_ref[...]) + g_open * scale) * gain_ref[...]
    wide = tok_ref[...].astype(F32)
    inverse = inverse_rms(wide)
    normed = wide * inverse
    back = inverse * (d_norm - normed * jnp.mean(d_norm * normed, axis=-1, keepdims=True))
    out_ref[...] = (g_resid + back).astype(BF)


def call(kernel, outs, flops, scratch=(), vmem=58, scalars=0, manual=0, hbm_outs=0):
    def run(*args):
        vmem_spec = pl.BlockSpec(memory_space=pltpu.VMEM)
        any_spec = pl.BlockSpec(memory_space=pl.ANY)
        specs = [vmem_spec] * (len(args) - scalars - manual) + [any_spec] * manual
        specs = [pl.BlockSpec(memory_space=pltpu.SMEM)] * scalars + specs
        out_specs = [vmem_spec] * (len(outs) - hbm_outs) + [any_spec] * hbm_outs
        moved = sum(a.size * a.dtype.itemsize for a in args)
        moved += sum(o.size * o.dtype.itemsize for o in outs)
        return pl.pallas_call(
            kernel,
            out_shape=outs if len(outs) > 1 else outs[0],
            in_specs=specs,
            out_specs=out_specs if len(outs) > 1 else out_specs[0],
            scratch_shapes=scratch,
            compiler_params=pltpu.CompilerParams(vmem_limit_bytes=vmem * 2**20),
            cost_estimate=pl.CostEstimate(flops=flops, bytes_accessed=moved, transcendentals=0),
            name=kernel.__name__,
        )(*args)

    return run


def struct(shape, dtype=BF):
    return jax.ShapeDtypeStruct(shape, dtype)


def exchange(chunked, axis_names):
    return lax.all_to_all(chunked, axis_names, 0, 0, tiled=True)


def seq_exchange(value):
    return exchange(value.reshape(CHUNKS, 8, HALF), SEQ).reshape(HALF, HALF)


def index_of(axis_names):
    return lax.axis_index(axis_names).astype(jnp.int32).reshape(1)


def shift(value, axis_name, step):
    return lax.ppermute(value, axis_name, [(i, (i + step) % 4) for i in range(4)])


def body(
    tokens, cotangent, first_factor, second_factor, norm_gain, gate_scale, gate_bias,
    mlp_gain, gate_weight, up_weight, down_weight,
):
    tok = tokens.reshape(ROWS, WIDTH)
    cot = cotangent.reshape(ROWS, WIDTH)
    first = first_factor.reshape(ROWS, ROWS)
    second = second_factor.reshape(ROWS, CHUNKS)
    gain1 = norm_gain.reshape(1, WIDTH)
    scale = gate_scale.reshape(1, WIDTH)
    bias = gate_bias.reshape(1, WIDTH)
    gain2 = mlp_gain.reshape(1, WIDTH)
    square = struct((HALF, HALF))

    normed, sec = call(norm_section, (struct((ROWS, WIDTH)), square), 10**9)(tok, first, gain1)
    m = call(prepare_mix, (square,), 10**8, vmem=12)(second)
    sec_cols = seq_exchange(sec)
    mixed_cols = call(mix, (square,), 3 * 10**8, vmem=12)(m, sec_cols)
    down, mixed_cols = lax.optimization_barrier((down_weight, mixed_cols))
    mixx = seq_exchange(mixed_cols)
    wt, gs = call(
        prepare_mlp, (struct((MB, 2 * HB, DB)), struct((MB, HB, ROWS))), 2 * 10**9, vmem=VM
    )(gate_weight, up_weight, down, cot)
    pieces_shape = struct((4, 3, 2, 2, 4, 32, DB))
    piece = struct((3, 2, 2, 4, 32, DB))
    gmix, g_resid, mixed, kept, *given = call(
        mlp,
        (square, struct((ROWS, WIDTH)), struct((ROWS, WIDTH)), pieces_shape)
        + (piece,) * 4,
        6 * 10**9,
        scratch=[
            pltpu.VMEM((HALF, HALF), BF),
            pltpu.VMEM((ROWS, WIDTH), BF),
            pltpu.VMEM((ROWS, WIDTH), BF),
            pltpu.VMEM((MB, 2 * HB, DB), BF),
            pltpu.VMEM((MB, HB, ROWS), BF),
            pltpu.VMEM((MB, DB, HB), BF),
            pltpu.VMEM((MB, DB, HB), BF),
            pltpu.VMEM((ROWS, WIDTH), BF),
            pltpu.VMEM((HALF, HALF), BF),
            pltpu.VMEM((ROWS, WIDTH), BF),
            pltpu.VMEM((ROWS, WIDTH), BF),
            pltpu.VMEM((ROWS, WIDTH), F32),
            pltpu.VMEM((ROWS, WIDTH), BF),
            pltpu.VMEM((MB, HB, ROWS), BF),
            pltpu.VMEM((2, 4, 3, 2, 2, 4, 32, DB), BF),
            pltpu.VMEM((MB, HB, DB), F32),
            pltpu.SemaphoreType.DMA((8, 2)),
            pltpu.SemaphoreType.DMA((21,)),
        ],
        scalars=1,
        manual=8,
        hbm_outs=8,
        vmem=VM,
    )(
        jnp.concatenate([index_of("core"), index_of("x")]), scale, bias, gain2,
        mixx, tok, normed, wt, gs, gate_weight, up_weight, cot,
    )

    gmix_cols = seq_exchange(gmix)
    gots = [lax.ppermute(term, "core", [(0, 1), (1, 0)]) for term in given]
    piece, half = struct((3, 2, 2, 4, 32, DB)), struct((3, 2, 4, 32, DB))
    pieces = call(sum_core, (piece, piece, half, half, piece), 10**6, vmem=12)(kept, *gots)
    own, up, far_up, far_down, down = pieces
    far_up, far_down = shift(far_up, "x", 1), shift(far_down, "x", 3)
    up, down = call(pass_on, (piece, piece), 10**6, vmem=12)(up, down, far_up, far_down)
    gmix_cols, up, down = lax.optimization_barrier((gmix_cols, up, down))
    gsec_cols = call(mix_back, (square,), 4 * 10**8, vmem=12)(second, gmix_cols)
    gsx = seq_exchange(gsec_cols)
    up, down = shift(up, "x", 1), shift(down, "x", 3)
    rows = call(sum_x, (struct((3, 2, 2, 32, DB)),) * 4, SUM_X_COST, vmem=12, scalars=1)(
        index_of("y"), own, up, down
    )
    gots = [shift(rows[step], "y", step) for step in (1, 2, 3)]
    parts = call(
        sum_y,
        (struct((3, 2, 2, 8, DB), F32),) * 4,
        10**6,
        scratch=[pltpu.VMEM((3, 2, 2, 32, DB), F32)],
        scalars=1,
        vmem=12,
    )(index_of("zl"), rows[0], *gots)
    line = [parts[0]] + [shift(parts[step], "zl", step) for step in (1, 2, 3)]
    gsx = lax.optimization_barrier((gsx, parts[0]))[0]
    second_t = call(second_grad, (struct((CHUNKS, ROWS)),), 5 * 10**8, vmem=12)(
        sec_cols, gmix_cols
    )
    gsec, kept, *given = call(
        first_grad,
        (struct((ROWS, WIDTH)), struct((2, 80, ROWS))) + (struct((80, ROWS)),) * 2,
        5 * 10**8,
        scratch=[pltpu.VMEM((4, 80, ROWS), BF)],
        scalars=1,
    )(index_of(DP), gsx, normed, second_t)
    grad_inputs = call(finish, (struct((ROWS, WIDTH)),), 2 * 10**8)(
        gsec, first, tok, g_resid, mixed, normed, scale, bias, gain1
    )

    gots = [lax.ppermute(piece, "core", [(0, 1), (1, 0)]) for piece in given]
    own, own_line, sent = call(
        sum_pair,
        (struct((80, ROWS), F32), struct((48, DB), F32), struct((112, ROWS))),
        10**6,
        scalars=1,
        vmem=12,
    )(index_of("zh"), kept, *gots, *line)
    sent = lax.ppermute(sent, "zh", [(0, 1), (1, 0)]).astype(F32)
    total = (own + sent[:80]) * (4 * WIDTH) ** (-0.5)
    whole = own_line + jnp.concatenate([sent[80:, :DB], sent[80:96, DB:]], axis=0)
    whole = whole * (4 * ROWS * CHUNKS) ** (-0.5)
    whole = whole.reshape(3, 2, 8, DB).transpose(0, 1, 3, 2)
    return (
        grad_inputs[None],
        total[:64].T[None],
        total[64:].T.reshape(CHUNKS, 4, 16),
        whole[0],
        whole[1],
        whole[2],
    )


def solution(mesh):
    fine = Mesh(mesh.devices.reshape(2, 2, 4, 4, 4), ("zh", "core", "y", "x", "zl"))
    placed = (
        P(DP, SEQ, None),
        P(DP, SEQ, None),
        P(SEQ, None, None),
        P(None, SEQ, None),
    ) + (P(),) * 7
    return jax.shard_map(
        body,
        mesh=fine,
        in_specs=placed,
        out_specs=(
            P(DP, SEQ, None),
            P(SEQ, None, DP),
            P(None, SEQ, DP),
            P(DP, None, SEQ),
            P(DP, None, SEQ),
            P(DP, None, SEQ),
        ),
        check_vma=False,
    )
```
